32 devices in a mesh: grp: 2 (over y), ctx: 8 (over z, x), head: 2 (over core).
Axes of the slice: x: 2, y: 2, z: 4, core: 2. Of those that a mesh axis runs over, the one named last changes fastest.
Arguments:
- query: bfloat16 [2048, 1024], P(('grp', 'ctx', 'head')), parts along dimension 0, may hold values from -6 to 6
- key: bfloat16 [2048, 1024], P(('grp', 'ctx', 'head')), parts along dimension 0, may hold values from -6 to 6
- value: bfloat16 [2048, 1024], P(('grp', 'ctx', 'head')), parts along dimension 0, may hold values from -6 to 6
- beta_logit: bfloat16 [2048, 8], P(('grp', 'ctx', 'head')), parts along dimension 0, may hold values from -10 to 11
- turn_ids: int32 [2048], P(('grp', 'ctx')), parts along dimension 0, may hold values from 0 to 3, never falling along the last dimension, each value on 1 to 512 neighbouring positions
- d_out: bfloat16 [2048, 1024], P(('grp', 'ctx', 'head')), parts along dimension 0, may hold values from -6 to 6
Outputs:
- out: bfloat16 [2048, 1024], P(('grp', 'ctx', 'head')), parts along dimension 0
- grad_query: bfloat16 [2048, 1024], P(('grp', 'ctx', 'head')), parts along dimension 0
- grad_key: bfloat16 [2048, 1024], P(('grp', 'ctx', 'head')), parts along dimension 0
- grad_value: bfloat16 [2048, 1024], P(('grp', 'ctx', 'head')), parts along dimension 0
- grad_beta: bfloat16 [2048, 8], P(('grp', 'ctx', 'head')), parts along dimension 0
The draws below stay inside these ranges and needn't reach their ends.
There are 2 independent parts, one for each index of `grp`. The reference program is written for one: setup_inputs(seed, part) draws one part's arguments, and reference() takes and returns one part's arrays. A program takes and returns all parts, laid end to end along the dimension named above; each array names one. Nothing has to cross between parts.
Inputs may be any that keep to these rules, and one draw needn't show every extreme that they name: turn_ids never decrease along the tokens; equal ids form one turn block of at most 512 tokens.
All inputs are finite; a program needn't handle non-finite values.
Results may differ from the reference program's by a relative error of at most 0.0012.
Values may be sent and summed in bfloat16 or wider, within the bound.
A program may use at most 256 MiB of HBM per device.

```python
import math
import jax
import jax.numpy as jnp
import numpy as np
from jax import lax

HEAD_COUNT = 8
DK = 128
BLOCK = 64
TOKEN_COUNT = 1024
TURNS = 4
TURN_MOST = 512


def draw_beta_logit(key, part):
    head_random_key, jitter_random_key, cluster_random_key = jax.random.split(key, 3)
    cluster_middles = jax.random.uniform(head_random_key, (HEAD_COUNT,), jnp.float32, -4.0, 3.0)
    random_jitter = jnp.clip(jax.random.normal(jitter_random_key, (TOKEN_COUNT, HEAD_COUNT), jnp.float32), -4.0, 4.0)
    token_clusters = jnp.where(jax.random.uniform(cluster_random_key, (TOKEN_COUNT, HEAD_COUNT), jnp.float32) < 0.01, 4.0, 0.0)
    return (cluster_middles[None, :] + random_jitter + token_clusters).astype(jnp.bfloat16)


def levels(rng, dims, shards, low, largest):
    loudness, own = 1.0, jax.random.fold_in(rng, 6)
    for dim, blocks in shards:
        draws = jnp.exp(jax.random.uniform(jax.random.fold_in(own, dim), (blocks,), jnp.float32, low / len(shards), largest / len(shards)))
        loudness = loudness * jnp.repeat(draws, dims[dim] // blocks).reshape([-1 if axis == dim else 1 for axis in range(len(dims))])
    return loudness


def split_up(count, total, reach, slope):
    loads = [(1 << 20) // math.isqrt(standing ** slope) + 1 for standing in range(2, count + 1)]
    surplus, given = total - reach - (count - 1), [1] * (count - 1)
    while surplus > 0:
        movable = [i for i in range(count - 1) if given[i] < reach]
        pool, left = sum([loads[i] for i in movable]), surplus
        for i in movable:
            more = min(reach - given[i], max(1, left * loads[i] // pool), surplus)
            given[i] = given[i] + more
            surplus = surplus - more
    return np.array([reach] + given)


def ragged(stream_key, number_of, total, bound, lean):
    if number_of == 2:
        one = jax.random.randint(stream_key, (), max(1, total - bound), min(bound, total - 1) + 1)
        return jnp.stack([one, total - one])
    lengths = jnp.asarray(split_up(number_of, total, bound, lean), jnp.int32)
    pairs = (number_of - 1) // 2
    source_of, receiver = lengths[1:1 + 2 * pairs:2], lengths[2:2 + 2 * pairs:2]
    room = jnp.minimum(source_of - 1, bound - receiver)
    moved = jax.random.randint(jax.random.fold_in(stream_key, 1), (pairs,), 0, 1 << 20) % (room + 1)
    lengths = lengths.at[1:1 + 2 * pairs:2].set(source_of - moved).at[2:2 + 2 * pairs:2].set(receiver + moved)
    return lengths[jax.random.permutation(jax.random.fold_in(stream_key, 2), number_of)]


def normal_values(rng, extent, scale, reach, cuts=(), held_as=jnp.bfloat16):
    values = scale * jax.random.normal(rng, extent, jnp.float32)
    if cuts:
        values = values * levels(rng, extent, cuts, -0.22, 0.18)
    return jnp.clip(values, -reach, reach).astype(held_as)


def setup_inputs(seed: int = 0, part: int = 0) -> dict:
    arg_keys = jax.random.split(jax.random.key(seed), 7)
    part_splits = jax.random.split(jax.random.fold_in(arg_keys[6], part), 7)
    return {
        "query": normal_values(part_splits[0], (TOKEN_COUNT, HEAD_COUNT * DK), 1.0, 6.0, ((0, 16),)),
        "key": normal_values(part_splits[1], (TOKEN_COUNT, HEAD_COUNT * DK), 1.0, 6.0, ((0, 16),)),
        "value": normal_values(part_splits[2], (TOKEN_COUNT, HEAD_COUNT * DK), 1.0, 6.0, ((0, 16),)),
        "beta_logit": draw_beta_logit(jax.random.fold_in(jax.random.fold_in(arg_keys[6], part), 71), part),
        "turn_ids": jnp.searchsorted(jnp.cumsum(ragged(part_splits[4], TURNS, TOKEN_COUNT, TURN_MOST, 2)), jnp.arange(TOKEN_COUNT), side="right").astype(jnp.int32),
        "d_out": normal_values(part_splits[5], (TOKEN_COUNT, HEAD_COUNT * DK), 1.0, 6.0, ((0, 16),)),
    }


highest = lax.Precision.HIGHEST
epsilon = 1e-06

def unit_rows(vectors):
    return vectors / jnp.sqrt(lax.optimization_barrier(jnp.sum(vectors * vectors, axis=-1, keepdims=True)) + epsilon)

def block_masks(turn_block, before):
    length = turn_block.shape[0]
    row_index = lax.broadcasted_iota(jnp.int32, (length, length), 0)
    col_index = lax.broadcasted_iota(jnp.int32, (length, length), 1)
    same_turn = turn_block[:, None] == turn_block[None, :]
    strict = jnp.where(same_turn & (row_index > col_index), 1.0, 0.0).astype(jnp.float32)
    inclusive = jnp.where(same_turn & (row_index >= col_index), 1.0, 0.0).astype(jnp.float32)
    continues = jnp.where(turn_block == before, 1.0, 0.0).astype(jnp.float32)
    in_last = jnp.where(turn_block == turn_block[length - 1], 1.0, 0.0).astype(jnp.float32)
    return (strict, inclusive, continues, in_last)

def block_state(state, keys, values, rates, turn_block, before):
    strict, inclusive, continues, in_last = block_masks(turn_block, before)
    length = keys.shape[0]
    key_gram = jnp.einsum('ihd,jhd->hij', keys, keys, precision=highest)
    scaled = jnp.transpose(rates)[:, :, None]
    system = jnp.eye(length, dtype=keys.dtype)[None] + scaled * key_gram * strict[None]
    predicted = jnp.einsum('ihd,hde->hie', keys, state, precision=highest)
    targets = scaled * (jnp.transpose(values, (1, 0, 2)) - continues[None, :, None] * predicted)
    updates = lax.linalg.triangular_solve(system, targets, left_side=True, lower=True)
    new_state = continues[length - 1] * state + jnp.einsum('ihd,hie->hde', keys, in_last[None, :, None] * updates, precision=highest)
    return (new_state, updates)

def block_output(state, queries, keys, updates, turn_block, before):
    strict, inclusive, continues, in_last = block_masks(turn_block, before)
    scores = jnp.einsum('ihd,jhd->hij', queries, keys, precision=highest) * inclusive[None]
    carried = jnp.einsum('ihd,hde->ihe', queries, state, precision=highest) * continues[:, None, None]
    within = jnp.einsum('hij,hje->ihe', scores, updates, precision=highest)
    return carried + within

def run_layer(query, key, value, beta_logit, turn_ids, first_before, start_state):
    tokens = query.shape[0]
    heads = beta_logit.shape[1]
    width = query.shape[1] // heads
    blocks = tokens // BLOCK
    queries = unit_rows(query.astype(jnp.float32).reshape(tokens, heads, width))
    keys = unit_rows(key.astype(jnp.float32).reshape(tokens, heads, width))
    values = value.astype(jnp.float32).reshape(tokens, heads, width)
    rates = 2.0 * jax.nn.sigmoid(beta_logit.astype(jnp.float32))
    turn_blocks = turn_ids.astype(jnp.int32).reshape(blocks, BLOCK)
    first = jnp.reshape(jnp.asarray(first_before).astype(jnp.int32), (1,))
    befores = jnp.concatenate([first, turn_blocks[:-1, BLOCK - 1].astype(jnp.int32)])

    def advance(state, inputs_block):
        query_block, key_block, value_block, rate_block, turn_block, before = inputs_block
        new_state, updates = block_state(state, key_block, value_block, rate_block, turn_block, before)
        outputs = block_output(state, query_block, key_block, updates, turn_block, before)
        return (new_state, outputs)
    final_state, outputs = lax.scan(jax.checkpoint(advance), start_state, (queries.reshape(blocks, BLOCK, heads, width), keys.reshape(blocks, BLOCK, heads, width), values.reshape(blocks, BLOCK, heads, width), rates.reshape(blocks, BLOCK, heads), turn_blocks, befores))
    return (outputs.reshape(tokens, heads * width), final_state)

def reference(query, key, value, beta_logit, turn_ids, d_out):
    start_state = jnp.zeros((HEAD_COUNT, DK, DK), jnp.float32)

    def forward(first_arg, second_arg, third_arg, fourth_arg):
        return run_layer(first_arg, second_arg, third_arg, fourth_arg, turn_ids, -1, start_state)[0]
    layer_out, pullback = jax.vjp(forward, query, key, value, beta_logit)
    gradients = pullback(d_out.astype(jnp.float32))
    return (layer_out.astype(jnp.bfloat16), gradients[0].astype(jnp.bfloat16), gradients[1].astype(jnp.bfloat16), gradients[2].astype(jnp.bfloat16), gradients[3].astype(jnp.bfloat16))
```

```python
import functools

import jax
import jax.numpy as jnp
from jax import lax
from jax.experimental import pallas as pl
from jax.experimental.pallas import tpu as pltpu
from jax.sharding import PartitionSpec as P

HEAD_COUNT = 8
DK = 128
epsilon = 1e-06
MESH = pl.DeviceIdType.MESH
f32 = jnp.float32
bf16 = jnp.bfloat16

NN = (((1,), (0,)), ((), ()))
NT = (((1,), (1,)), ((), ()))
TN = (((0,), (0,)), ((), ()))


def split(x):
    if x.dtype == bf16:
        return (x, None)
    high = x.astype(bf16)
    return (high, (x - high.astype(f32)).astype(bf16))


def product(a, b, dims=NN):
    left, right = [a[0]], [b[0]]
    if a[1] is not None:
        left.append(a[1])
        right.append(b[0])
    if b[1] is not None:
        left.append(a[0])
        right.append(b[1])
    (ca,), (cb,) = dims[0]
    left = jnp.concatenate(left, axis=ca) if len(left) > 1 else left[0]
    right = jnp.concatenate(right, axis=cb) if len(right) > 1 else right[0]
    return lax.dot_general(left, right, dims, preferred_element_type=f32)


def stack(a, b, axis=0):
    low = None
    if a[1] is not None or b[1] is not None:
        zero_a = jnp.zeros_like(a[0]) if a[1] is None else a[1]
        zero_b = jnp.zeros_like(b[0]) if b[1] is None else b[1]
        low = jnp.concatenate([zero_a, zero_b], axis=axis)
    return (jnp.concatenate([a[0], b[0]], axis=axis), low)


def unit(x):
    scale = lax.rsqrt(jnp.sum(x * x, axis=1, keepdims=True) + epsilon)
    return x * scale, scale


def column(row):
    return jnp.transpose(jnp.broadcast_to(row, (row.shape[1], row.shape[1])))


def kernel(
    groups, sub, ids_ref, logit_ref, q_ref, k_ref, v_ref, d_ref,
    out_ref, gq_ref, gk_ref, gv_ref, gb_ref,
    small_src, small, kb, vb, qb, db, yb, gqb, gkb, gvb, rate_src, rate_in,
    ahead_src, ahead, back_src, back,
    send_in, recv_in, send_out, recv_out, send_state, recv_state, local_sem,
):
    count = HEAD_COUNT
    cores = count // sub
    tokens = q_ref.shape[0]
    chunk = tokens * cores
    ctx, core = lax.axis_index("ctx"), lax.axis_index("head")
    group = ctx // sub
    me = (ctx % sub) * cores + core

    def device(member):
        return {"ctx": group * sub + member // cores, "head": member % cores}

    def others():
        return [lax.rem(me + d, count) for d in range(1, count)]

    def columns(member):
        return pl.ds(pl.multiple_of(member * DK, DK), DK)

    def rows(member):
        return pl.ds(pl.multiple_of(member * tokens, tokens), tokens)

    barrier = pltpu.get_barrier_semaphore()
    for other in others():
        pl.semaphore_signal(barrier, inc=1, device_id=device(other), device_id_type=MESH)
    waits = count - 1
    if groups > 1:
        @pl.when(group > 0)
        def _():
            pl.semaphore_signal(barrier, inc=1, device_id={"ctx": ctx - sub}, device_id_type=MESH)

        @pl.when(group < groups - 1)
        def _():
            pl.semaphore_signal(barrier, inc=1, device_id={"ctx": ctx + sub}, device_id_type=MESH)

        waits = waits + (group + groups - 1) // groups + (groups - 1 - group + groups - 1) // groups

    arrays = [(k_ref, kb), (v_ref, vb), (q_ref, qb), (d_ref, db)]
    own = [
        pltpu.make_async_copy(src.at[:, columns(me)], dst.at[rows(me), :], local_sem.at[i])
        for i, (src, dst) in enumerate(arrays)
    ]
    for copy in own:
        copy.start()

    logits = jnp.pad(logit_ref[...].astype(f32), ((0, 0), (0, DK - count)))
    placed = jnp.concatenate([jnp.where(core == c, logits, 0.0) for c in range(cores)], axis=0)
    small_src[0:8, :] = jnp.transpose(placed)[0:8, :]
    small_src[8:16, :] = jnp.broadcast_to(ids_ref[...].astype(f32), (8, chunk))
    small[me] = small_src[...]

    pl.semaphore_wait(barrier, waits)

    def copy_small(other, source):
        return pltpu.make_async_remote_copy(
            src_ref=small_src, dst_ref=small.at[source], send_sem=send_in.at[4, other],
            recv_sem=recv_in.at[4, source], device_id=device(other), device_id_type=MESH)

    def copy_in(i, other, source):
        src, dst = arrays[i]
        return pltpu.make_async_remote_copy(
            src_ref=src.at[:, columns(other)], dst_ref=dst.at[rows(source), :], send_sem=send_in.at[i, other],
            recv_sem=recv_in.at[i, source], device_id=device(other), device_id_type=MESH)

    for other in others():
        copy_in(0, other, me).start()
    for other in others():
        copy_small(other, me).start()
    for i in (1, 2, 3):
        for other in others():
            copy_in(i, other, me).start()

    def arrived(i):
        own[i].wait()
        for other in others():
            copy_in(i, other, other).wait_recv()

    row_index = lax.broadcasted_iota(jnp.int32, (chunk, chunk), 0)
    col_index = lax.broadcasted_iota(jnp.int32, (chunk, chunk), 1)
    eye = jnp.where(row_index == col_index, 1.0, 0.0).astype(f32)
    lower = row_index > col_index
    lower_equal = row_index >= col_index
    chunks = range(sub)
    part = [pl.ds(c * chunk, chunk) for c in chunks]

    for other in others():
        copy_small(other, other).wait_recv()
    pick = lax.broadcasted_iota(jnp.int32, (8, chunk), 0) == me
    ids, same, logit, rate, cont, in_last, last_cont = [], [], [], [], [], [], []
    before = None
    for c in chunks:
        block = sum(small[cores * c + p, 0:8, :] for p in range(cores))
        logit.append(column(jnp.sum(jnp.where(pick, block, 0.0), axis=0, keepdims=True)))
        rate.append(2.0 / (1.0 + jnp.exp(-logit[c])))
        id_row = small[cores * c, 8:9, :]
        id_col = column(id_row)
        ids.append(id_row)
        same.append(id_col == id_row)
        first = id_row[:, 0:1] if before is None else before
        cont.append(jnp.where(id_col == first, 1.0, 0.0).astype(f32))
        before = id_row[:, chunk - 1:chunk]
        in_last.append(jnp.where(id_col == before, 1.0, 0.0).astype(f32))
        last_cont.append(jnp.where(before == first, 1.0, 0.0).astype(f32))

    arrived(0)
    keys, key_scale, key, inverse = [], [], [], []
    system = []
    for c in chunks:
        unit_keys, scale = unit(kb[part[c], :].astype(f32))
        keys.append(unit_keys)
        key_scale.append(scale)
        key.append(split(unit_keys))
        gram = product(key[c], key[c], NT)
        system.append(rate[c] * jnp.where(same[c] & lower, gram, 0.0))
    size = 1
    while size < chunk:
        rb, cb = row_index // size, col_index // size
        off = (rb // 2 == cb // 2) & (rb > cb)
        if size == 1:
            inverse = [eye - jnp.where(off, system[c], 0.0) for c in chunks]
        else:
            pieces = [split(inverse[c]) for c in chunks]
            steps = [product(split(jnp.where(off, system[c], 0.0)), pieces[c]) for c in chunks]
            inverse = [inverse[c] - product(pieces[c], split(steps[c])) for c in chunks]
        size = size * 2
    inv = [split(inverse[c]) for c in chunks]

    arrived(1)
    joint, key_last, trans, offset = [], [], [], []
    for c in chunks:
        right = jnp.concatenate([rate[c] * cont[c] * keys[c], rate[c] * vb[part[c], :].astype(f32)], axis=1)
        joint.append(product(inv[c], split(right)))
    joint_s = [split(joint[c]) for c in chunks]
    for c in chunks:
        last = in_last[c].astype(bf16)
        key_last.append((key[c][0] * last, key[c][1] * last))
        both = product(key_last[c], joint_s[c], TN)
        trans.append(split(last_cont[c] * eye - both[:, :DK]))
        offset.append(both[:, DK:])

    if groups > 1:
        state = offset[0]
        for c in chunks[1:]:
            state = product(trans[c], split(state)) + offset[c]
        ahead_src[0:DK, :] = state
        ahead_src[DK:DK + 8, :] = jnp.broadcast_to(ids[-1][:, chunk - 1:chunk], (8, DK))

        def copy_ahead():
            return pltpu.make_async_remote_copy(
                src_ref=ahead_src, dst_ref=ahead, send_sem=send_state.at[0], recv_sem=recv_state.at[0],
                device_id={"ctx": ctx + sub}, device_id_type=MESH)

        def copy_back():
            return pltpu.make_async_remote_copy(
                src_ref=back_src, dst_ref=back, send_sem=send_state.at[1], recv_sem=recv_state.at[1],
                device_id={"ctx": ctx - sub}, device_id_type=MESH)

        @pl.when(group < groups - 1)
        def _():
            copy_ahead().start()

    arrived(2)
    queries, query_scale, query, scores = [], [], [], []
    for c in chunks:
        unit_queries, scale = unit(qb[part[c], :].astype(f32))
        queries.append(unit_queries)
        query_scale.append(scale)
        query.append(split(unit_queries))
        scores.append(split(jnp.where(same[c] & lower_equal, product(query[c], key[c], NT), 0.0)))
    reach, within = [], []
    for c in chunks:
        both = product(scores[c], joint_s[c])
        reach.append(split(cont[c] * queries[c] - both[:, :DK]))
        within.append(both[:, DK:])

    arrived(3)
    upstream = [(db[part[c], :], None) for c in chunks]
    response = [product(reach[c], upstream[c], TN) for c in chunks]
    if groups > 1:
        adjoint = response[-1]
        for c in reversed(chunks[:-1]):
            adjoint = product(trans[c], split(adjoint), TN) + response[c]
        back_src[0:DK, :] = adjoint
        back_src[DK:DK + 8, :] = jnp.broadcast_to(ids[0][:, 0:1], (8, DK))

        @pl.when(group > 0)
        def _():
            copy_back().start()

    direct = [product(scores[c], upstream[c], TN) for c in chunks]

    if groups > 1:
        @pl.when(group > 0)
        def _():
            copy_ahead().wait_recv()

        @pl.when(group == 0)
        def _():
            ahead[...] = jnp.zeros_like(ahead)

        @pl.when(group < groups - 1)
        def _():
            copy_back().wait_recv()

        @pl.when(group == groups - 1)
        def _():
            back[...] = jnp.zeros_like(back)

        first_state = jnp.where(ahead[DK:DK + 1, :] == ids[0][:, 0:1], ahead[0:DK, :], 0.0)
        last_adjoint = jnp.where(back[DK:DK + 1, :] == ids[-1][:, chunk - 1:chunk], back[0:DK, :], 0.0)
    else:
        first_state = jnp.zeros((DK, DK), f32)
        last_adjoint = jnp.zeros((DK, DK), f32)

    states = [split(first_state)]
    for c in chunks[:-1]:
        states.append(split(product(trans[c], states[c]) + offset[c]))
    adjoints = [None] * sub
    adjoints[-1] = split(last_adjoint)
    for c in reversed(chunks[:-1]):
        adjoints[c] = split(product(trans[c + 1], adjoints[c + 1], TN) + response[c + 1])

    def send_result(i, source_buffer, target):
        for other in others():
            copy_out(i, source_buffer, target, other, me).start()

    def copy_out(i, source_buffer, target, other, source):
        return pltpu.make_async_remote_copy(
            src_ref=source_buffer.at[rows(other), :], dst_ref=target.at[:, columns(source)],
            send_sem=send_out.at[i, other], recv_sem=recv_out.at[i, source],
            device_id=device(other), device_id_type=MESH)

    updates = []
    for c in chunks:
        weights = (joint_s[c][0][:, :DK], joint_s[c][1][:, :DK])
        both = product(stack(reach[c], weights), states[c])
        yb[part[c], :] = (within[c] + both[:chunk]).astype(bf16)
        updates.append(joint[c][:, DK:] - both[chunk:])
    send_result(0, yb, out_ref)
    update = [split(updates[c]) for c in chunks]

    targets = [product(inv[c], split(direct[c] + product(key_last[c], adjoints[c])), TN) for c in chunks]
    value_grads = [rate[c] * targets[c] for c in chunks]
    for c in chunks:
        gvb[part[c], :] = value_grads[c].astype(bf16)
    send_result(1, gvb, gv_ref)

    for c in chunks:
        lead = stack(split(value_grads[c]), upstream[c])
        both = product(lead, stack(update[c], states[c]), NT)
        gram_grad = jnp.where(same[c] & lower, both[:chunk, :chunk], 0.0)
        score_grad = split(jnp.where(same[c] & lower_equal, both[chunk:, :chunk], 0.0))
        around = split(-(gram_grad + jnp.transpose(gram_grad)))
        near = product(stack(score_grad, around), key[c])
        query_grad = near[:chunk] + cont[c] * both[chunk:, chunk:]
        key_grad = (
            near[chunk:] - cont[c] * both[:chunk, chunk:] + product(score_grad, query[c], TN)
            + in_last[c] * product(update[c], adjoints[c], NT)
        )
        query_grad = query_scale[c] * (
            query_grad - queries[c] * jnp.sum(queries[c] * query_grad, axis=1, keepdims=True))
        key_grad = key_scale[c] * (
            key_grad - keys[c] * jnp.sum(keys[c] * key_grad, axis=1, keepdims=True))
        gqb[part[c], :] = query_grad.astype(bf16)
        gkb[part[c], :] = key_grad.astype(bf16)
        logit_grad = jnp.sum(targets[c] * updates[c], axis=1, keepdims=True) / (1.0 + jnp.exp(logit[c]))
        rate_src[c] = jnp.transpose(logit_grad)[0:8, :]
    send_result(2, gqb, gq_ref)
    send_result(3, gkb, gk_ref)

    def copy_rate(other, source):
        return pltpu.make_async_remote_copy(
            src_ref=rate_src.at[other // cores], dst_ref=rate_in.at[source], send_sem=send_out.at[4, other],
            recv_sem=recv_out.at[4, source], device_id=device(other), device_id_type=MESH)

    for other in others():
        copy_rate(other, me).start()

    results = [(yb, out_ref), (gvb, gv_ref), (gqb, gq_ref), (gkb, gk_ref)]
    for buffer, target in results:
        target[:, columns(me)] = buffer[rows(me), :]
    rate_in[me] = rate_src[me // cores]

    for other in others():
        copy_rate(other, other).wait_recv()
    head_row = lax.broadcasted_iota(jnp.int32, (8, chunk), 0)
    gathered = sum(jnp.where(head_row == h, rate_in[h], 0.0) for h in range(count))
    spread = jnp.transpose(jnp.concatenate([gathered, jnp.zeros((chunk - 8, chunk), f32)], axis=0))
    mine = sum(jnp.where(core == p, spread[p * tokens:(p + 1) * tokens, :], 0.0) for p in range(cores))
    gb_ref[...] = mine[:, :count].astype(bf16)

    for i, (buffer, target) in enumerate(results):
        for other in others():
            copy_out(i, buffer, target, other, other).wait_recv()
    for other in others():
        copy_small(other, me).wait_send()
        copy_rate(other, me).wait_send()
        for i in range(4):
            copy_in(i, other, me).wait_send()
            copy_out(i, results[i][0], results[i][1], other, me).wait_send()
    if groups > 1:
        @pl.when(group < groups - 1)
        def _():
            copy_ahead().wait_send()

        @pl.when(group > 0)
        def _():
            copy_back().wait_send()


def on_device(query, key, value, beta_logit, turn_ids, d_out):
    cores = lax.axis_size("head")
    sub = HEAD_COUNT // cores
    groups = lax.axis_size("ctx") // sub
    tokens = query.shape[0]
    chunk = tokens * cores
    total = chunk * sub
    wide = jax.ShapeDtypeStruct(query.shape, bf16)
    vmem = pl.BlockSpec(memory_space=pltpu.VMEM)
    anywhere = pl.BlockSpec(memory_space=pl.ANY)
    dma = pltpu.SemaphoreType.DMA
    buffer = pltpu.VMEM((total, DK), bf16)
    state = pltpu.VMEM((DK + 8, DK), f32)
    return pl.pallas_call(
        functools.partial(kernel, groups, sub),
        out_shape=(wide, wide, wide, wide, jax.ShapeDtypeStruct(beta_logit.shape, bf16)),
        in_specs=[vmem, vmem] + [anywhere] * 4,
        out_specs=(vmem,) * 5,
        scratch_shapes=[
            pltpu.VMEM((16, chunk), f32),
            pltpu.VMEM((HEAD_COUNT, 16, chunk), f32),
            buffer, buffer, buffer, buffer,
            buffer, buffer, buffer, buffer,
            pltpu.VMEM((sub, 8, chunk), f32),
            pltpu.VMEM((HEAD_COUNT, 8, chunk), f32),
            state, state, state, state,
            dma((5, HEAD_COUNT)), dma((5, HEAD_COUNT)), dma((5, HEAD_COUNT)), dma((5, HEAD_COUNT)),
            dma((2,)), dma((2,)), dma((4,)),
        ],
        compiler_params=pltpu.CompilerParams(
            collective_id=0, has_side_effects=True, vmem_limit_bytes=48 * 1024 * 1024),
        cost_estimate=pl.CostEstimate(flops=1_500_000_000, bytes_accessed=2_000_000, transcendentals=100_000),
    )(turn_ids.reshape(1, chunk), beta_logit, query, key, value, d_out)


def solution(mesh):
    tokens = P(("grp", "ctx", "head"), None)
    return jax.shard_map(
        on_device,
        mesh=mesh,
        in_specs=(tokens, tokens, tokens, tokens, P(("grp", "ctx")), tokens),
        out_specs=(tokens,) * 5,
        check_vma=False,
    )
```

```python
import functools

import jax
import jax.numpy as jnp
from jax import lax
from jax.experimental import pallas as pl
from jax.experimental.pallas import tpu as pltpu
from jax.sharding import PartitionSpec as P

HEAD_COUNT = 8
DK = 128
epsilon = 1e-06
MESH = pl.DeviceIdType.MESH
f32 = jnp.float32
bf16 = jnp.bfloat16

NN = (((1,), (0,)), ((), ()))
NT = (((1,), (1,)), ((), ()))
TN = (((0,), (0,)), ((), ()))


def split(x):
    if x.dtype == bf16:
        return (x, None)
    high = x.astype(bf16)
    return (high, (x - high.astype(f32)).astype(bf16))


def product(a, b, dims=NN):
    left, right = [a[0]], [b[0]]
    if a[1] is not None:
        left.append(a[1])
        right.append(b[0])
    if b[1] is not None:
        left.append(a[0])
        right.append(b[1])
    (ca,), (cb,) = dims[0]
    left = jnp.concatenate(left, axis=ca) if len(left) > 1 else left[0]
    right = jnp.concatenate(right, axis=cb) if len(right) > 1 else right[0]
    return lax.dot_general(left, right, dims, preferred_element_type=f32)


def stack(a, b, axis=0):
    low = None
    if a[1] is not None or b[1] is not None:
        zero_a = jnp.zeros_like(a[0]) if a[1] is None else a[1]
        zero_b = jnp.zeros_like(b[0]) if b[1] is None else b[1]
        low = jnp.concatenate([zero_a, zero_b], axis=axis)
    return (jnp.concatenate([a[0], b[0]], axis=axis), low)


def unit(x):
    scale = lax.rsqrt(jnp.sum(x * x, axis=1, keepdims=True) + epsilon)
    return x * scale, scale


def column(row):
    return jnp.transpose(jnp.broadcast_to(row, (row.shape[1], row.shape[1])))


def kernel(
    groups, sub, ids_hbm, logit_hbm, q_ref, k_ref, v_ref, d_ref,
    out_ref, gq_ref, gk_ref, gv_ref, gb_ref,
    ids_ref, logit_ref, small_src, small, kb, vb, qb, db, yb, gqb, gkb, gvb, rate_src, rate_in,
    ahead_src, ahead, back_src, back,
    send_in, recv_in, send_out, recv_out, send_state, recv_state, local_sem,
):
    count = HEAD_COUNT
    cores = count // sub
    tokens = q_ref.shape[0]
    chunk = tokens * cores
    ctx, core = lax.axis_index("ctx"), lax.axis_index("head")
    group = ctx // sub
    me = (ctx % sub) * cores + core

    def device(member):
        return {"ctx": group * sub + member // cores, "head": member % cores}

    def others():
        return [lax.rem(me + d, count) for d in range(1, count)]

    def columns(member):
        return pl.ds(pl.multiple_of(member * DK, DK), DK)

    def rows(member):
        return pl.ds(pl.multiple_of(member * tokens, tokens), tokens)

    barrier = pltpu.get_barrier_semaphore()
    for other in others():
        pl.semaphore_signal(barrier, inc=1, device_id=device(other), device_id_type=MESH)
    waits = count - 1
    if groups > 1:
        @pl.when(group > 0)
        def _():
            pl.semaphore_signal(barrier, inc=1, device_id={"ctx": ctx - sub}, device_id_type=MESH)

        @pl.when(group < groups - 1)
        def _():
            pl.semaphore_signal(barrier, inc=1, device_id={"ctx": ctx + sub}, device_id_type=MESH)

        waits = waits + (group + groups - 1) // groups + (groups - 1 - group + groups - 1) // groups

    arrays = [(k_ref, kb), (v_ref, vb), (q_ref, qb), (d_ref, db)]
    own = [
        pltpu.make_async_copy(src.at[:, columns(me)], dst.at[rows(me), :], local_sem.at[i])
        for i, (src, dst) in enumerate(arrays)
    ]
    early = [
        pltpu.make_async_copy(ids_hbm, ids_ref, local_sem.at[4]),
        pltpu.make_async_copy(logit_hbm, logit_ref, local_sem.at[5]),
    ]
    for copy in early + own:
        copy.start()
    for copy in early:
        copy.wait()

    logits = logit_ref[...].astype(f32)
    small_src[0:8, :] = jnp.concatenate([jnp.where(core == c, logits, 0.0) for c in range(cores)], axis=1)
    small_src[8:16, :] = jnp.broadcast_to(ids_ref[...].astype(f32), (8, chunk))
    small[me] = small_src[...]

    pl.semaphore_wait(barrier, waits)

    def copy_small(other, source):
        return pltpu.make_async_remote_copy(
            src_ref=small_src, dst_ref=small.at[source], send_sem=send_in.at[4, other],
            recv_sem=recv_in.at[4, source], device_id=device(other), device_id_type=MESH)

    def copy_in(i, other, source):
        src, dst = arrays[i]
        return pltpu.make_async_remote_copy(
            src_ref=src.at[:, columns(other)], dst_ref=dst.at[rows(source), :], send_sem=send_in.at[i, other],
            recv_sem=recv_in.at[i, source], device_id=device(other), device_id_type=MESH)

    for other in others():
        copy_in(0, other, me).start()
    for other in others():
        copy_small(other, me).start()
    for i in (1, 2, 3):
        for other in others():
            copy_in(i, other, me).start()

    def arrived(i):
        own[i].wait()
        for other in others():
            copy_in(i, other, other).wait_recv()

    row_index = lax.broadcasted_iota(jnp.int32, (chunk, chunk), 0)
    col_index = lax.broadcasted_iota(jnp.int32, (chunk, chunk), 1)
    eye = jnp.where(row_index == col_index, 1.0, 0.0).astype(f32)
    lower = row_index > col_index
    lower_equal = row_index >= col_index
    chunks = range(sub)
    part = [pl.ds(c * chunk, chunk) for c in chunks]

    for other in others():
        copy_small(other, other).wait_recv()
    pick = lax.broadcasted_iota(jnp.int32, (8, chunk), 0) == me
    ids, same, logit, rate, cont, in_last, last_cont = [], [], [], [], [], [], []
    before = None
    for c in chunks:
        block = sum(small[cores * c + p, 0:8, :] for p in range(cores))
        logit.append(column(jnp.sum(jnp.where(pick, block, 0.0), axis=0, keepdims=True)))
        rate.append(2.0 / (1.0 + jnp.exp(-logit[c])))
        id_row = small[cores * c, 8:9, :]
        id_col = column(id_row)
        ids.append(id_row)
        same.append(id_col == id_row)
        first = id_row[:, 0:1] if before is None else before
        cont.append(jnp.where(id_col == first, 1.0, 0.0).astype(f32))
        before = id_row[:, chunk - 1:chunk]
        in_last.append(jnp.where(id_col == before, 1.0, 0.0).astype(f32))
        last_cont.append(jnp.where(before == first, 1.0, 0.0).astype(f32))

    arrived(0)
    keys, key_scale, key, inverse = [], [], [], []
    system = []
    for c in chunks:
        unit_keys, scale = unit(kb[part[c], :].astype(f32))
        keys.append(unit_keys)
        key_scale.append(scale)
        key.append(split(unit_keys))
        gram = product(key[c], key[c], NT)
        system.append(rate[c] * jnp.where(same[c] & lower, gram, 0.0))
    size = 1
    while size < chunk:
        rb, cb = row_index // size, col_index // size
        off = (rb // 2 == cb // 2) & (rb > cb)
        if size == 1:
            inverse = [eye - jnp.where(off, system[c], 0.0) for c in chunks]
        else:
            pieces = [split(inverse[c]) for c in chunks]
            steps = [product(split(jnp.where(off, system[c], 0.0)), pieces[c]) for c in chunks]
            inverse = [inverse[c] - product(pieces[c], split(steps[c])) for c in chunks]
        size = size * 2
    inv = [split(inverse[c]) for c in chunks]

    arrived(1)
    joint, key_last, trans, offset = [], [], [], []
    for c in chunks:
        right = jnp.concatenate([rate[c] * cont[c] * keys[c], rate[c] * vb[part[c], :].astype(f32)], axis=1)
        joint.append(product(inv[c], split(right)))
    joint_s = [split(joint[c]) for c in chunks]
    for c in chunks:
        last = in_last[c].astype(bf16)
        key_last.append((key[c][0] * last, key[c][1] * last))
        both = product(key_last[c], joint_s[c], TN)
        trans.append(split(last_cont[c] * eye - both[:, :DK]))
        offset.append(both[:, DK:])

    if groups > 1:
        state = offset[0]
        for c in chunks[1:]:
            state = product(trans[c], split(state)) + offset[c]
        ahead_src[0:DK, :] = state
        ahead_src[DK:DK + 8, :] = jnp.broadcast_to(ids[-1][:, chunk - 1:chunk], (8, DK))

        def copy_ahead():
            return pltpu.make_async_remote_copy(
                src_ref=ahead_src, dst_ref=ahead, send_sem=send_state.at[0], recv_sem=recv_state.at[0],
                device_id={"ctx": ctx + sub}, device_id_type=MESH)

        def copy_back():
            return pltpu.make_async_remote_copy(
                src_ref=back_src, dst_ref=back, send_sem=send_state.at[1], recv_sem=recv_state.at[1],
                device_id={"ctx": ctx - sub}, device_id_type=MESH)

        @pl.when(group < groups - 1)
        def _():
            copy_ahead().start()

    arrived(2)
    queries, query_scale, query, scores = [], [], [], []
    for c in chunks:
        unit_queries, scale = unit(qb[part[c], :].astype(f32))
        queries.append(unit_queries)
        query_scale.append(scale)
        query.append(split(unit_queries))
        scores.append(split(jnp.where(same[c] & lower_equal, product(query[c], key[c], NT), 0.0)))
    reach, within = [], []
    for c in chunks:
        both = product(scores[c], joint_s[c])
        reach.append(split(cont[c] * queries[c] - both[:, :DK]))
        within.append(both[:, DK:])

    arrived(3)
    upstream = [(db[part[c], :], None) for c in chunks]
    response = [product(reach[c], upstream[c], TN) for c in chunks]
    if groups > 1:
        adjoint = response[-1]
        for c in reversed(chunks[:-1]):
            adjoint = product(trans[c], split(adjoint), TN) + response[c]
        back_src[0:DK, :] = adjoint
        back_src[DK:DK + 8, :] = jnp.broadcast_to(ids[0][:, 0:1], (8, DK))

        @pl.when(group > 0)
        def _():
            copy_back().start()

    direct = [product(scores[c], upstream[c], TN) for c in chunks]

    if groups > 1:
        @pl.when(group > 0)
        def _():
            copy_ahead().wait_recv()

        @pl.when(group == 0)
        def _():
            ahead[...] = jnp.zeros_like(ahead)

        @pl.when(group < groups - 1)
        def _():
            copy_back().wait_recv()

        @pl.when(group == groups - 1)
        def _():
            back[...] = jnp.zeros_like(back)

        first_state = jnp.where(ahead[DK:DK + 1, :] == ids[0][:, 0:1], ahead[0:DK, :], 0.0)
        last_adjoint = jnp.where(back[DK:DK + 1, :] == ids[-1][:, chunk - 1:chunk], back[0:DK, :], 0.0)
    else:
        first_state = jnp.zeros((DK, DK), f32)
        last_adjoint = jnp.zeros((DK, DK), f32)

    states = [split(first_state)]
    for c in chunks[:-1]:
        states.append(split(product(trans[c], states[c]) + offset[c]))
    adjoints = [None] * sub
    adjoints[-1] = split(last_adjoint)
    for c in reversed(chunks[:-1]):
        adjoints[c] = split(product(trans[c + 1], adjoints[c + 1], TN) + response[c + 1])

    def send_result(i, source_buffer, target):
        for other in others():
            copy_out(i, source_buffer, target, other, me).start()

    def copy_out(i, source_buffer, target, other, source):
        return pltpu.make_async_remote_copy(
            src_ref=source_buffer.at[rows(other), :], dst_ref=target.at[:, columns(source)],
            send_sem=send_out.at[i, other], recv_sem=recv_out.at[i, source],
            device_id=device(other), device_id_type=MESH)

    updates = []
    for c in chunks:
        weights = (joint_s[c][0][:, :DK], joint_s[c][1][:, :DK])
        both = product(stack(reach[c], weights), states[c])
        yb[part[c], :] = (within[c] + both[:chunk]).astype(bf16)
        updates.append(joint[c][:, DK:] - both[chunk:])
    send_result(0, yb, out_ref)
    update = [split(updates[c]) for c in chunks]

    targets = [product(inv[c], split(direct[c] + product(key_last[c], adjoints[c])), TN) for c in chunks]
    value_grads = [rate[c] * targets[c] for c in chunks]
    for c in chunks:
        gvb[part[c], :] = value_grads[c].astype(bf16)
    send_result(1, gvb, gv_ref)

    for c in chunks:
        lead = stack(split(value_grads[c]), upstream[c])
        both = product(lead, stack(update[c], states[c]), NT)
        gram_grad = jnp.where(same[c] & lower, both[:chunk, :chunk], 0.0)
        score_grad = split(jnp.where(same[c] & lower_equal, both[chunk:, :chunk], 0.0))
        around = split(-(gram_grad + jnp.transpose(gram_grad)))
        near = product(stack(score_grad, around), key[c])
        query_grad = near[:chunk] + cont[c] * both[chunk:, chunk:]
        key_grad = (
            near[chunk:] - cont[c] * both[:chunk, chunk:] + product(score_grad, query[c], TN)
            + in_last[c] * product(update[c], adjoints[c], NT)
        )
        query_grad = query_scale[c] * (
            query_grad - queries[c] * jnp.sum(queries[c] * query_grad, axis=1, keepdims=True))
        key_grad = key_scale[c] * (
            key_grad - keys[c] * jnp.sum(keys[c] * key_grad, axis=1, keepdims=True))
        gqb[part[c], :] = query_grad.astype(bf16)
        gkb[part[c], :] = key_grad.astype(bf16)
        logit_grad = jnp.sum(targets[c] * updates[c], axis=1, keepdims=True) / (1.0 + jnp.exp(logit[c]))
        rate_src[c] = jnp.transpose(logit_grad)[0:8, :]
    send_result(2, gqb, gq_ref)
    send_result(3, gkb, gk_ref)

    def copy_rate(other, source):
        return pltpu.make_async_remote_copy(
            src_ref=rate_src.at[other // cores], dst_ref=rate_in.at[source], send_sem=send_out.at[4, other],
            recv_sem=recv_out.at[4, source], device_id=device(other), device_id_type=MESH)

    for other in others():
        copy_rate(other, me).start()

    results = [(yb, out_ref), (gvb, gv_ref), (gqb, gq_ref), (gkb, gk_ref)]
    for buffer, target in results:
        target[:, columns(me)] = buffer[rows(me), :]
    rate_in[me] = rate_src[me // cores]

    for other in others():
        copy_rate(other, other).wait_recv()
    head_row = lax.broadcasted_iota(jnp.int32, (8, chunk), 0)
    gathered = sum(jnp.where(head_row == h, rate_in[h], 0.0) for h in range(count))
    mine = sum(jnp.where(core == p, gathered[:, p * tokens:(p + 1) * tokens], 0.0) for p in range(cores))
    gb_ref[...] = mine.astype(bf16)

    for i, (buffer, target) in enumerate(results):
        for other in others():
            copy_out(i, buffer, target, other, other).wait_recv()
    for other in others():
        copy_small(other, me).wait_send()
        copy_rate(other, me).wait_send()
        for i in range(4):
            copy_in(i, other, me).wait_send()
            copy_out(i, results[i][0], results[i][1], other, me).wait_send()
    if groups > 1:
        @pl.when(group < groups - 1)
        def _():
            copy_ahead().wait_send()

        @pl.when(group > 0)
        def _():
            copy_back().wait_send()


def place(*refs):
    count = len(refs) // 2
    copies = [
        pltpu.make_async_copy(refs[i], refs[count + i], refs[-1].at[i]) for i in range(count)
    ]
    for copy in copies:
        copy.start()
    for copy in copies:
        copy.wait()


def on_device(query, key, value, beta_logit, turn_ids, d_out):
    cores = lax.axis_size("head")
    sub = HEAD_COUNT // cores
    groups = lax.axis_size("ctx") // sub
    tokens = query.shape[0]
    chunk = tokens * cores
    total = chunk * sub
    wide = jax.ShapeDtypeStruct(query.shape, bf16)
    vmem = pl.BlockSpec(memory_space=pltpu.VMEM)
    anywhere = pl.BlockSpec(memory_space=pl.ANY)
    dma = pltpu.SemaphoreType.DMA
    buffer = pltpu.VMEM((total, DK), bf16)
    state = pltpu.VMEM((DK + 8, DK), f32)
    hbm = pl.BlockSpec(memory_space=pltpu.HBM)
    narrow = jax.ShapeDtypeStruct(beta_logit.shape[::-1], bf16)
    results = pl.pallas_call(
        functools.partial(kernel, groups, sub),
        out_shape=(wide, wide, wide, wide, narrow),
        in_specs=[hbm] * 6,
        out_specs=(vmem,) * 5,
        scratch_shapes=[
            pltpu.VMEM((1, chunk), jnp.int32),
            pltpu.VMEM(narrow.shape, bf16),
            pltpu.VMEM((16, chunk), f32),
            pltpu.VMEM((HEAD_COUNT, 16, chunk), f32),
            buffer, buffer, buffer, buffer,
            buffer, buffer, buffer, buffer,
            pltpu.VMEM((sub, 8, chunk), f32),
            pltpu.VMEM((HEAD_COUNT, 8, chunk), f32),
            state, state, state, state,
            dma((5, HEAD_COUNT)), dma((5, HEAD_COUNT)), dma((5, HEAD_COUNT)), dma((5, HEAD_COUNT)),
            dma((2,)), dma((2,)), dma((6,)),
        ],
        compiler_params=pltpu.CompilerParams(
            collective_id=0, has_side_effects=True, vmem_limit_bytes=48 * 1024 * 1024),
        cost_estimate=pl.CostEstimate(flops=1_500_000_000, bytes_accessed=2_000_000, transcendentals=100_000),
    )(*(pltpu.with_memory_space_constraint(x, pltpu.HBM) for x in (turn_ids.reshape(1, chunk), beta_logit.T, query, key, value, d_out)))
    results = pl.pallas_call(
        place,
        out_shape=(wide, wide, wide, wide, narrow),
        in_specs=[anywhere] * 5,
        out_specs=(hbm,) * 5,
        scratch_shapes=[dma((5,))],
        cost_estimate=pl.CostEstimate(flops=0, bytes_accessed=1_000_000, transcendentals=0),
    )(*(pltpu.with_memory_space_constraint(x, pltpu.VMEM) for x in results))
    return (*results[:4], results[4].T)


def solution(mesh):
    tokens = P(("grp", "ctx", "head"), None)
    return jax.shard_map(
        on_device,
        mesh=mesh,
        in_specs=(tokens, tokens, tokens, tokens, P(("grp", "ctx")), tokens),
        out_specs=(tokens,) * 5,
        check_vma=False,
    )
```

```python
import functools

import jax
import jax.numpy as jnp
from jax import lax
from jax.experimental import pallas as pl
from jax.experimental.pallas import tpu as pltpu
from jax.sharding import PartitionSpec as P

HEAD_COUNT = 8
DK = 128
epsilon = 1e-06
MESH = pl.DeviceIdType.MESH
f32 = jnp.float32
bf16 = jnp.bfloat16

NN = (((1,), (0,)), ((), ()))
NT = (((1,), (1,)), ((), ()))
TN = (((0,), (0,)), ((), ()))


def split(x):
    if x.dtype == bf16:
        return (x, None)
    high = x.astype(bf16)
    return (high, (x - high.astype(f32)).astype(bf16))


def product(a, b, dims=NN):
    left, right = [a[0]], [b[0]]
    if a[1] is not None:
        left.append(a[1])
        right.append(b[0])
    if b[1] is not None:
        left.append(a[0])
        right.append(b[1])
    (ca,), (cb,) = dims[0]
    left = jnp.concatenate(left, axis=ca) if len(left) > 1 else left[0]
    right = jnp.concatenate(right, axis=cb) if len(right) > 1 else right[0]
    return lax.dot_general(left, right, dims, preferred_element_type=f32)


def stack(a, b, axis=0):
    low = None
    if a[1] is not None or b[1] is not None:
        zero_a = jnp.zeros_like(a[0]) if a[1] is None else a[1]
        zero_b = jnp.zeros_like(b[0]) if b[1] is None else b[1]
        low = jnp.concatenate([zero_a, zero_b], axis=axis)
    return (jnp.concatenate([a[0], b[0]], axis=axis), low)


def unit(x):
    scale = lax.rsqrt(jnp.sum(x * x, axis=1, keepdims=True) + epsilon)
    return x * scale, scale


def column(row):
    return jnp.transpose(jnp.broadcast_to(row, (row.shape[1], row.shape[1])))


def kernel(
    groups, sub, ids_hbm, logit_hbm, q_ref, k_ref, v_ref, d_ref,
    first_out, second_out, gb_ref,
    ids_ref, logit_ref, first_src, second_src, first_in, second_in, first_back, second_back,
    ahead_src, ahead, back_src, back,
    send_in, recv_in, send_out, recv_out, send_state, recv_state, local_sem,
):
    count = HEAD_COUNT
    cores = count // sub
    tokens = q_ref.shape[0]
    chunk = tokens * cores
    ctx, core = lax.axis_index("ctx"), lax.axis_index("head")
    group = ctx // sub
    me = (ctx % sub) * cores + core

    def device(member):
        return {"ctx": group * sub + member // cores, "head": member % cores}

    def others():
        return [lax.rem(me + d, count) for d in range(1, count)]

    def columns(member):
        return pl.ds(pl.multiple_of(member * DK, DK), DK)

    def rows(member):
        return pl.ds(pl.multiple_of(member * tokens, tokens), tokens)

    barrier = pltpu.get_barrier_semaphore()
    for other in others():
        pl.semaphore_signal(barrier, inc=1, device_id=device(other), device_id_type=MESH)
    waits = count - 1
    if groups > 1:
        @pl.when(group > 0)
        def _():
            pl.semaphore_signal(barrier, inc=1, device_id={"ctx": ctx - sub}, device_id_type=MESH)

        @pl.when(group < groups - 1)
        def _():
            pl.semaphore_signal(barrier, inc=1, device_id={"ctx": ctx + sub}, device_id_type=MESH)

        waits = waits + (group + groups - 1) // groups + (groups - 1 - group + groups - 1) // groups

    own = [
        pltpu.make_async_copy(src, dst.at[pl.ds(start, tokens), :], local_sem.at[i])
        for i, (src, dst, start) in enumerate([
            (k_ref, first_src, 0), (v_ref, second_src, 0),
            (q_ref, second_src, tokens), (d_ref, second_src, 2 * tokens)])
    ]
    early = [
        pltpu.make_async_copy(ids_hbm, ids_ref, local_sem.at[4]),
        pltpu.make_async_copy(logit_hbm, logit_ref, local_sem.at[5]),
    ]
    for copy in early + own:
        copy.start()
    for copy in early:
        copy.wait()

    logits = logit_ref[...].astype(f32)
    logits = jnp.concatenate([jnp.where(core == c, logits, 0.0) for c in range(cores)], axis=1)
    turns = jnp.broadcast_to(ids_ref[...].astype(f32), (8, chunk))
    extra = jnp.concatenate([logits, turns], axis=0).astype(bf16)
    for member in range(count):
        first_src[tokens:tokens + 16, member * DK:(member + 1) * DK] = extra

    def copy_in(i, other, source):
        src, dst = [(first_src, first_in), (second_src, second_in)][i]
        return pltpu.make_async_remote_copy(
            src_ref=src.at[:, columns(other)], dst_ref=dst.at[source], send_sem=send_in.at[i, other],
            recv_sem=recv_in.at[i, source], device_id=device(other), device_id_type=MESH)

    own[0].wait()
    pl.semaphore_wait(barrier, waits)
    for other in others():
        copy_in(0, other, me).start()
    for copy in own[1:]:
        copy.wait()
    for other in others():
        copy_in(1, other, me).start()
    first_in[me] = first_src[:, columns(me)]
    second_in[me] = second_src[:, columns(me)]

    def arrived(i):
        for other in others():
            copy_in(i, other, other).wait_recv()

    def block_of(buffer, start, c):
        return jnp.concatenate([buffer[cores * c + p, start:start + tokens, :] for p in range(cores)], axis=0)

    def put(buffer, start, c, value):
        for p in range(cores):
            buffer[cores * c + p, start:start + tokens, :] = value[p * tokens:(p + 1) * tokens].astype(bf16)

    row_index = lax.broadcasted_iota(jnp.int32, (chunk, chunk), 0)
    col_index = lax.broadcasted_iota(jnp.int32, (chunk, chunk), 1)
    eye = jnp.where(row_index == col_index, 1.0, 0.0).astype(f32)
    lower = row_index > col_index
    lower_equal = row_index >= col_index
    chunks = range(sub)

    arrived(0)
    pick = lax.broadcasted_iota(jnp.int32, (8, chunk), 0) == me
    ids, same, logit, rate, cont, in_last, last_cont = [], [], [], [], [], [], []
    before = None
    for c in chunks:
        extras = [first_in[cores * c + p, tokens:tokens + 16, :].astype(f32) for p in range(cores)]
        block = sum(extras[p][0:8, :] for p in range(cores))
        logit.append(column(jnp.sum(jnp.where(pick, block, 0.0), axis=0, keepdims=True)))
        rate.append(2.0 / (1.0 + jnp.exp(-logit[c])))
        id_row = extras[0][8:9, :]
        id_col = column(id_row)
        ids.append(id_row)
        same.append(id_col == id_row)
        first = id_row[:, 0:1] if before is None else before
        cont.append(jnp.where(id_col == first, 1.0, 0.0).astype(f32))
        before = id_row[:, chunk - 1:chunk]
        in_last.append(jnp.where(id_col == before, 1.0, 0.0).astype(f32))
        last_cont.append(jnp.where(before == first, 1.0, 0.0).astype(f32))

    keys, key_scale, key, inverse = [], [], [], []
    system = []
    for c in chunks:
        unit_keys, scale = unit(block_of(first_in, 0, c).astype(f32))
        keys.append(unit_keys)
        key_scale.append(scale)
        key.append(split(unit_keys))
        gram = product(key[c], key[c], NT)
        system.append(rate[c] * jnp.where(same[c] & lower, gram, 0.0))
    size = 1
    while size < chunk:
        rb, cb = row_index // size, col_index // size
        off = (rb // 2 == cb // 2) & (rb > cb)
        if size == 1:
            inverse = [eye - jnp.where(off, system[c], 0.0) for c in chunks]
        else:
            pieces = [split(inverse[c]) for c in chunks]
            steps = [product(split(jnp.where(off, system[c], 0.0)), pieces[c]) for c in chunks]
            inverse = [inverse[c] - product(pieces[c], split(steps[c])) for c in chunks]
        size = size * 2
    inv = [split(inverse[c]) for c in chunks]

    arrived(1)
    joint, key_last, trans, offset = [], [], [], []
    for c in chunks:
        right = jnp.concatenate([rate[c] * cont[c] * keys[c], rate[c] * block_of(second_in, 0, c).astype(f32)], axis=1)
        joint.append(product(inv[c], split(right)))
    joint_s = [split(joint[c]) for c in chunks]
    for c in chunks:
        last = in_last[c].astype(bf16)
        key_last.append((key[c][0] * last, key[c][1] * last))
        both = product(key_last[c], joint_s[c], TN)
        trans.append(split(last_cont[c] * eye - both[:, :DK]))
        offset.append(both[:, DK:])

    if groups > 1:
        state = offset[0]
        for c in chunks[1:]:
            state = product(trans[c], split(state)) + offset[c]
        ahead_src[0:DK, :] = state
        ahead_src[DK:DK + 8, :] = jnp.broadcast_to(ids[-1][:, chunk - 1:chunk], (8, DK))

        def copy_ahead():
            return pltpu.make_async_remote_copy(
                src_ref=ahead_src, dst_ref=ahead, send_sem=send_state.at[0], recv_sem=recv_state.at[0],
                device_id={"ctx": ctx + sub}, device_id_type=MESH)

        def copy_back():
            return pltpu.make_async_remote_copy(
                src_ref=back_src, dst_ref=back, send_sem=send_state.at[1], recv_sem=recv_state.at[1],
                device_id={"ctx": ctx - sub}, device_id_type=MESH)

        @pl.when(group < groups - 1)
        def _():
            copy_ahead().start()

    queries, query_scale, query, scores = [], [], [], []
    for c in chunks:
        unit_queries, scale = unit(block_of(second_in, tokens, c).astype(f32))
        queries.append(unit_queries)
        query_scale.append(scale)
        query.append(split(unit_queries))
        scores.append(split(jnp.where(same[c] & lower_equal, product(query[c], key[c], NT), 0.0)))
    reach, within = [], []
    for c in chunks:
        both = product(scores[c], joint_s[c])
        reach.append(split(cont[c] * queries[c] - both[:, :DK]))
        within.append(both[:, DK:])

    upstream = [(block_of(second_in, 2 * tokens, c), None) for c in chunks]
    response = [product(reach[c], upstream[c], TN) for c in chunks]
    if groups > 1:
        adjoint = response[-1]
        for c in reversed(chunks[:-1]):
            adjoint = product(trans[c], split(adjoint), TN) + response[c]
        back_src[0:DK, :] = adjoint
        back_src[DK:DK + 8, :] = jnp.broadcast_to(ids[0][:, 0:1], (8, DK))

        @pl.when(group > 0)
        def _():
            copy_back().start()

    direct = [product(scores[c], upstream[c], TN) for c in chunks]

    if groups > 1:
        @pl.when(group > 0)
        def _():
            copy_ahead().wait_recv()

        @pl.when(group == 0)
        def _():
            ahead[...] = jnp.zeros_like(ahead)

        first_state = jnp.where(ahead[DK:DK + 1, :] == ids[0][:, 0:1], ahead[0:DK, :], 0.0)
    else:
        first_state = jnp.zeros((DK, DK), f32)

    states = [split(first_state)]
    for c in chunks[:-1]:
        states.append(split(product(trans[c], states[c]) + offset[c]))

    results = [(first_back, first_out), (second_back, second_out)]

    def copy_out(i, other, source):
        return pltpu.make_async_remote_copy(
            src_ref=results[i][0].at[other], dst_ref=results[i][1].at[:, columns(source)],
            send_sem=send_out.at[i, other], recv_sem=recv_out.at[i, source],
            device_id=device(other), device_id_type=MESH)

    def send_result(i):
        for other in others():
            copy_out(i, other, me).start()

    updates = []
    for c in chunks:
        weights = (joint_s[c][0][:, :DK], joint_s[c][1][:, :DK])
        both = product(stack(reach[c], weights), states[c])
        put(first_back, 0, c, within[c] + both[:chunk])
        updates.append(joint[c][:, DK:] - both[chunk:])
    update = [split(updates[c]) for c in chunks]

    both_side, score_grad = [], []
    for c in chunks:
        both_side.append(stack(update[c], states[c]))
        both = product(upstream[c], both_side[c], NT)
        score_grad.append(split(jnp.where(same[c] & lower_equal, both[:, :chunk], 0.0)))
        query_grad = product(score_grad[c], key[c]) + cont[c] * both[:, chunk:]
        query_grad = query_scale[c] * (
            query_grad - queries[c] * jnp.sum(queries[c] * query_grad, axis=1, keepdims=True))
        put(first_back, tokens, c, query_grad)
    send_result(0)
    cross = [product(score_grad[c], query[c], TN) for c in chunks]

    if groups > 1:
        @pl.when(group < groups - 1)
        def _():
            copy_back().wait_recv()

        @pl.when(group == groups - 1)
        def _():
            back[...] = jnp.zeros_like(back)

        last_adjoint = jnp.where(back[DK:DK + 1, :] == ids[-1][:, chunk - 1:chunk], back[0:DK, :], 0.0)
    else:
        last_adjoint = jnp.zeros((DK, DK), f32)
    adjoints = [None] * sub
    adjoints[-1] = split(last_adjoint)
    for c in reversed(chunks[:-1]):
        adjoints[c] = split(product(trans[c + 1], adjoints[c + 1], TN) + response[c + 1])

    targets = [product(inv[c], split(direct[c] + product(key_last[c], adjoints[c])), TN) for c in chunks]
    value_grads = [rate[c] * targets[c] for c in chunks]
    for c in chunks:
        put(second_back, 0, c, value_grads[c])

    for c in chunks:
        both = product(split(value_grads[c]), both_side[c], NT)
        gram_grad = jnp.where(same[c] & lower, both[:, :chunk], 0.0)
        around = split(-(gram_grad + jnp.transpose(gram_grad)))
        key_grad = (
            product(around, key[c]) - cont[c] * both[:, chunk:] + cross[c]
            + in_last[c] * product(update[c], adjoints[c], NT)
        )
        key_grad = key_scale[c] * (
            key_grad - keys[c] * jnp.sum(keys[c] * key_grad, axis=1, keepdims=True))
        put(second_back, tokens, c, key_grad)
        logit_grad = jnp.sum(targets[c] * updates[c], axis=1, keepdims=True) / (1.0 + jnp.exp(logit[c]))
        logit_rows = jnp.transpose(logit_grad)[0:16, :].astype(bf16)
        for p in range(cores):
            second_back[cores * c + p, 2 * tokens:2 * tokens + 16, :] = logit_rows
    send_result(1)

    for i, (buffer, target) in enumerate(results):
        target[:, columns(me)] = buffer[me]
        for other in others():
            copy_out(i, other, other).wait_recv()
    head_row = lax.broadcasted_iota(jnp.int32, (8, chunk), 0)
    gathered = sum(
        jnp.where(head_row == h, second_out[2 * tokens:2 * tokens + 16, h * DK:(h + 1) * DK].astype(f32)[0:8], 0.0)
        for h in range(count))
    mine = sum(jnp.where(core == p, gathered[:, p * tokens:(p + 1) * tokens], 0.0) for p in range(cores))
    gb_ref[...] = mine.astype(bf16)

    for other in others():
        for i in range(2):
            copy_in(i, other, me).wait_send()
            copy_out(i, other, me).wait_send()
    if groups > 1:
        @pl.when(group < groups - 1)
        def _():
            copy_ahead().wait_send()

        @pl.when(group > 0)
        def _():
            copy_back().wait_send()


def place(first, second, narrow, out, gq, gk, gv, gb, sem):
    tokens = out.shape[0]
    head, tail = pl.ds(0, tokens), pl.ds(tokens, tokens)
    pairs = [
        (first.at[head, :], out), (first.at[tail, :], gq), (second.at[tail, :], gk),
        (second.at[head, :], gv), (narrow, gb)]
    copies = [pltpu.make_async_copy(src, dst, sem.at[i]) for i, (src, dst) in enumerate(pairs)]
    for copy in copies:
        copy.start()
    for copy in copies:
        copy.wait()


def on_device(query, key, value, beta_logit, turn_ids, d_out):
    cores = lax.axis_size("head")
    sub = HEAD_COUNT // cores
    groups = lax.axis_size("ctx") // sub
    tokens = query.shape[0]
    chunk = tokens * cores
    width = query.shape[1]
    wide = jax.ShapeDtypeStruct(query.shape, bf16)
    vmem = pl.BlockSpec(memory_space=pltpu.VMEM)
    anywhere = pl.BlockSpec(memory_space=pl.ANY)
    dma = pltpu.SemaphoreType.DMA
    rows = (tokens + 16, 3 * tokens, 2 * tokens, 2 * tokens + 16)
    state = pltpu.VMEM((DK + 8, DK), f32)
    hbm = pl.BlockSpec(memory_space=pltpu.HBM)
    narrow = jax.ShapeDtypeStruct(beta_logit.shape[::-1], bf16)
    results = pl.pallas_call(
        functools.partial(kernel, groups, sub),
        out_shape=(*(jax.ShapeDtypeStruct((n, width), bf16) for n in rows[2:]), narrow),
        in_specs=[hbm] * 6,
        out_specs=(vmem,) * 3,
        scratch_shapes=[
            pltpu.VMEM((1, chunk), jnp.int32),
            pltpu.VMEM(narrow.shape, bf16),
            *(pltpu.VMEM((n, width), bf16) for n in rows[:2]),
            *(pltpu.VMEM((HEAD_COUNT, n, DK), bf16) for n in rows),
            state, state, state, state,
            *(dma((2, HEAD_COUNT)) for _ in range(4)),
            dma((2,)), dma((2,)), dma((6,)),
        ],
        compiler_params=pltpu.CompilerParams(
            collective_id=0, has_side_effects=True, vmem_limit_bytes=48 * 1024 * 1024),
        cost_estimate=pl.CostEstimate(flops=1_500_000_000, bytes_accessed=2_000_000, transcendentals=100_000),
    )(*(pltpu.with_memory_space_constraint(x, pltpu.HBM) for x in (turn_ids.reshape(1, chunk), beta_logit.T, query, key, value, d_out)))
    results = pl.pallas_call(
        place,
        out_shape=(wide, wide, wide, wide, narrow),
        in_specs=[anywhere] * 3,
        out_specs=(hbm,) * 5,
        scratch_shapes=[dma((5,))],
        cost_estimate=pl.CostEstimate(flops=0, bytes_accessed=1_000_000, transcendentals=0),
    )(*(pltpu.with_memory_space_constraint(x, pltpu.VMEM) for x in results))
    return (*results[:4], results[4].T)


def solution(mesh):
    tokens = P(("grp", "ctx", "head"), None)
    return jax.shard_map(
        on_device,
        mesh=mesh,
        in_specs=(tokens, tokens, tokens, tokens, P(("grp", "ctx")), tokens),
        out_specs=(tokens,) * 5,
        check_vma=False,
    )
```

```python
import functools

import jax
import jax.numpy as jnp
from jax import lax
from jax.experimental import pallas as pl
from jax.experimental.pallas import tpu as pltpu
from jax.sharding import PartitionSpec as P

HEAD_COUNT = 8
DK = 128
epsilon = 1e-06
MESH = pl.DeviceIdType.MESH
f32 = jnp.float32
bf16 = jnp.bfloat16

NN = (((1,), (0,)), ((), ()))
NT = (((1,), (1,)), ((), ()))
TN = (((0,), (0,)), ((), ()))


def split(x):
    if x.dtype == bf16:
        return (x, None)
    high = x.astype(bf16)
    return (high, (x - high.astype(f32)).astype(bf16))


def product(a, b, dims=NN):
    left, right = [a[0]], [b[0]]
    if a[1] is not None:
        left.append(a[1])
        right.append(b[0])
    if b[1] is not None:
        left.append(a[0])
        right.append(b[1])
    (ca,), (cb,) = dims[0]
    left = jnp.concatenate(left, axis=ca) if len(left) > 1 else left[0]
    right = jnp.concatenate(right, axis=cb) if len(right) > 1 else right[0]
    return lax.dot_general(left, right, dims, preferred_element_type=f32)


def stack(a, b, axis=0):
    low = None
    if a[1] is not None or b[1] is not None:
        zero_a = jnp.zeros_like(a[0]) if a[1] is None else a[1]
        zero_b = jnp.zeros_like(b[0]) if b[1] is None else b[1]
        low = jnp.concatenate([zero_a, zero_b], axis=axis)
    return (jnp.concatenate([a[0], b[0]], axis=axis), low)


def unit(x):
    scale = lax.rsqrt(jnp.sum(x * x, axis=1, keepdims=True) + epsilon)
    return x * scale, scale


def column(row):
    return jnp.transpose(jnp.broadcast_to(row, (row.shape[1], row.shape[1])))


def kernel(
    groups, sub, ids_hbm, logit_hbm, q_ref, k_ref, v_ref, d_ref,
    first_out, second_out, gb_ref,
    ids_ref, logit_ref, first_src, second_src, first_in, second_in, first_back, second_back,
    ahead_src, ahead, back_src, back,
    send_in, recv_in, send_out, recv_out, send_state, recv_state, local_sem,
):
    count = HEAD_COUNT
    cores = count // sub
    tokens = q_ref.shape[0]
    chunk = tokens * cores
    ctx, core = lax.axis_index("ctx"), lax.axis_index("head")
    group = ctx // sub
    me = (ctx % sub) * cores + core

    def device(member):
        return {"ctx": group * sub + member // cores, "head": member % cores}

    def others():
        return [lax.rem(me + d, count) for d in range(1, count)]

    def columns(member):
        return pl.ds(pl.multiple_of(member * DK, DK), DK)

    def rows(member):
        return pl.ds(pl.multiple_of(member * tokens, tokens), tokens)

    barrier = pltpu.get_barrier_semaphore()
    for other in others():
        pl.semaphore_signal(barrier, inc=1, device_id=device(other), device_id_type=MESH)
    waits = count - 1
    if groups > 1:
        @pl.when(group > 0)
        def _():
            pl.semaphore_signal(barrier, inc=1, device_id={"ctx": ctx - sub}, device_id_type=MESH)

        @pl.when(group < groups - 1)
        def _():
            pl.semaphore_signal(barrier, inc=1, device_id={"ctx": ctx + sub}, device_id_type=MESH)

        waits = waits + (group + groups - 1) // groups + (groups - 1 - group + groups - 1) // groups

    own = [
        pltpu.make_async_copy(src, dst.at[pl.ds(start, tokens), :], local_sem.at[i])
        for i, (src, dst, start) in enumerate([
            (k_ref, first_src, 0), (q_ref, second_src, 0),
            (v_ref, second_src, tokens), (d_ref, second_src, 2 * tokens)])
    ]
    early = [
        pltpu.make_async_copy(ids_hbm, ids_ref, local_sem.at[4]),
        pltpu.make_async_copy(logit_hbm, logit_ref, local_sem.at[5]),
    ]
    for copy in early + own:
        copy.start()
    for copy in early:
        copy.wait()

    logits = logit_ref[...].astype(f32)
    logits = jnp.concatenate([jnp.where(core == c, logits, 0.0) for c in range(cores)], axis=1)
    turns = jnp.broadcast_to(ids_ref[...].astype(f32), (8, chunk))
    extra = jnp.concatenate([logits, turns], axis=0).astype(bf16)
    for member in range(count):
        first_src[tokens:tokens + 16, member * DK:(member + 1) * DK] = extra

    def copy_in(i, other, source):
        src, dst, start, size = [
            (first_src, first_in, 0, tokens + 16), (second_src, second_in, 0, tokens),
            (second_src, second_in, tokens, 2 * tokens)][i]
        return pltpu.make_async_remote_copy(
            src_ref=src.at[pl.ds(start, size), columns(other)], dst_ref=dst.at[source, pl.ds(start, size), :], send_sem=send_in.at[i, other],
            recv_sem=recv_in.at[i, source], device_id=device(other), device_id_type=MESH)

    own[0].wait()
    pl.semaphore_wait(barrier, waits)
    for other in others():
        copy_in(0, other, me).start()
    for copy in own[1:]:
        copy.wait()
    for i in (1, 2):
        for other in others():
            copy_in(i, other, me).start()
    first_in[me] = first_src[:, columns(me)]
    second_in[me] = second_src[:, columns(me)]

    def arrived(i):
        for other in others():
            copy_in(i, other, other).wait_recv()

    def block_of(buffer, start, c):
        return jnp.concatenate([buffer[cores * c + p, start:start + tokens, :] for p in range(cores)], axis=0)

    def put(buffer, start, c, value):
        for p in range(cores):
            buffer[cores * c + p, start:start + tokens, :] = value[p * tokens:(p + 1) * tokens].astype(bf16)

    row_index = lax.broadcasted_iota(jnp.int32, (chunk, chunk), 0)
    col_index = lax.broadcasted_iota(jnp.int32, (chunk, chunk), 1)
    eye = jnp.where(row_index == col_index, 1.0, 0.0).astype(f32)
    lower = row_index > col_index
    lower_equal = row_index >= col_index
    chunks = range(sub)

    arrived(0)
    pick = lax.broadcasted_iota(jnp.int32, (8, chunk), 0) == me
    ids, same, logit, rate, cont, in_last, last_cont = [], [], [], [], [], [], []
    before = None
    for c in chunks:
        extras = [first_in[cores * c + p, tokens:tokens + 16, :].astype(f32) for p in range(cores)]
        block = sum(extras[p][0:8, :] for p in range(cores))
        logit.append(column(jnp.sum(jnp.where(pick, block, 0.0), axis=0, keepdims=True)))
        rate.append(2.0 / (1.0 + jnp.exp(-logit[c])))
        id_row = extras[0][8:9, :]
        id_col = column(id_row)
        ids.append(id_row)
        same.append(id_col == id_row)
        first = id_row[:, 0:1] if before is None else before
        cont.append(jnp.where(id_col == first, 1.0, 0.0).astype(f32))
        before = id_row[:, chunk - 1:chunk]
        in_last.append(jnp.where(id_col == before, 1.0, 0.0).astype(f32))
        last_cont.append(jnp.where(before == first, 1.0, 0.0).astype(f32))

    keys, key_scale, key, inverse = [], [], [], []
    system = []
    for c in chunks:
        unit_keys, scale = unit(block_of(first_in, 0, c).astype(f32))
        keys.append(unit_keys)
        key_scale.append(scale)
        key.append(split(unit_keys))
        gram = product(key[c], key[c], NT)
        system.append(rate[c] * jnp.where(same[c] & lower, gram, 0.0))
    size = 1
    while size < chunk:
        rb, cb = row_index // size, col_index // size
        off = (rb // 2 == cb // 2) & (rb > cb)
        if size == 1:
            inverse = [eye - jnp.where(off, system[c], 0.0) for c in chunks]
        else:
            pieces = [split(inverse[c]) for c in chunks]
            steps = [product(split(jnp.where(off, system[c], 0.0)), pieces[c]) for c in chunks]
            inverse = [inverse[c] - product(pieces[c], split(steps[c])) for c in chunks]
        size = size * 2
    inv = [split(inverse[c]) for c in chunks]

    weight, key_last, trans = [], [], []
    for c in chunks:
        weight.append(split(product(inv[c], split(rate[c] * cont[c] * keys[c]))))
        last = in_last[c].astype(bf16)
        key_last.append((key[c][0] * last, key[c][1] * last))
        trans.append(split(last_cont[c] * eye - product(key_last[c], weight[c], TN)))
    from_start = [None, trans[0]]
    for c in chunks[1:-1]:
        from_start.append(split(product(trans[c], from_start[c])))
    to_end = [None] * sub
    to_end[-2] = trans[-1]
    for c in reversed(chunks[:-2]):
        to_end[c] = split(product(to_end[c + 1], trans[c + 1]))

    arrived(1)
    queries, query_scale, query, scores, reach = [], [], [], [], []
    for c in chunks:
        unit_queries, scale = unit(block_of(second_in, 0, c).astype(f32))
        queries.append(unit_queries)
        query_scale.append(scale)
        query.append(split(unit_queries))
        scores.append(split(jnp.where(same[c] & lower_equal, product(query[c], key[c], NT), 0.0)))
    for c in chunks:
        reach.append(split(cont[c] * queries[c] - product(scores[c], weight[c])))

    arrived(2)
    upstream = [(block_of(second_in, 2 * tokens, c), None) for c in chunks]
    response = [product(reach[c], upstream[c], TN) for c in chunks]
    fresh, offset = [], []
    for c in chunks:
        fresh.append(product(inv[c], split(rate[c] * block_of(second_in, tokens, c).astype(f32))))
    fresh_s = [split(fresh[c]) for c in chunks]
    offset = [product(key_last[c], fresh_s[c], TN) for c in chunks]
    response_s = [split(response[c]) for c in chunks]
    offset_s = [split(offset[c]) for c in chunks]

    if groups > 1:
        def copy_ahead():
            return pltpu.make_async_remote_copy(
                src_ref=ahead_src, dst_ref=ahead, send_sem=send_state.at[0], recv_sem=recv_state.at[0],
                device_id={"ctx": ctx + sub}, device_id_type=MESH)

        def copy_back():
            return pltpu.make_async_remote_copy(
                src_ref=back_src, dst_ref=back, send_sem=send_state.at[1], recv_sem=recv_state.at[1],
                device_id={"ctx": ctx - sub}, device_id_type=MESH)

        ahead_src[0:DK, :] = offset[-1] + sum(product(to_end[c], offset_s[c]) for c in chunks[:-1])
        ahead_src[DK:DK + 8, :] = jnp.broadcast_to(ids[-1][:, chunk - 1:chunk], (8, DK))

        @pl.when(group < groups - 1)
        def _():
            copy_ahead().start()

        back_src[0:DK, :] = response[0] + sum(product(from_start[c], response_s[c], TN) for c in chunks[1:])
        back_src[DK:DK + 8, :] = jnp.broadcast_to(ids[0][:, 0:1], (8, DK))

        @pl.when(group > 0)
        def _():
            copy_back().start()

    within = [product(scores[c], fresh_s[c]) for c in chunks]
    own_state = [None, offset[0]]
    for c in chunks[1:-1]:
        own_state.append(product(trans[c], split(own_state[c])) + offset[c])
    own_adjoint = [None] * sub
    own_adjoint[-2] = response[-1]
    for c in reversed(chunks[:-2]):
        own_adjoint[c] = product(trans[c + 1], split(own_adjoint[c + 1]), TN) + response[c + 1]
    direct = [product(scores[c], upstream[c], TN) for c in chunks]

    if groups > 1:
        @pl.when(group > 0)
        def _():
            copy_ahead().wait_recv()

        @pl.when(group == 0)
        def _():
            ahead[...] = jnp.zeros_like(ahead)

        first_state = jnp.where(ahead[DK:DK + 1, :] == ids[0][:, 0:1], ahead[0:DK, :], 0.0)
    else:
        first_state = jnp.zeros((DK, DK), f32)

    states = [split(first_state)]
    for c in chunks[1:]:
        states.append(split(product(from_start[c], states[0]) + own_state[c]))

    results = [(first_back, first_out), (second_back, second_out)]

    def copy_out(i, other, source):
        src, dst, start, size = [
            (first_back, first_out, 0, 2 * tokens), (second_back, second_out, 0, tokens),
            (second_back, second_out, tokens, tokens + 16)][i]
        return pltpu.make_async_remote_copy(
            src_ref=src.at[other, pl.ds(start, size), :], dst_ref=dst.at[pl.ds(start, size), columns(source)],
            send_sem=send_out.at[i, other], recv_sem=recv_out.at[i, source],
            device_id=device(other), device_id_type=MESH)

    def send_result(i):
        for other in others():
            copy_out(i, other, me).start()

    updates = []
    for c in chunks:
        both = product(stack(reach[c], weight[c]), states[c])
        put(first_back, 0, c, within[c] + both[:chunk])
        updates.append(fresh[c] - both[chunk:])
    update = [split(updates[c]) for c in chunks]

    both_side, score_grad = [], []
    for c in chunks:
        both_side.append(stack(update[c], states[c]))
        both = product(upstream[c], both_side[c], NT)
        score_grad.append(split(jnp.where(same[c] & lower_equal, both[:, :chunk], 0.0)))
        query_grad = product(score_grad[c], key[c]) + cont[c] * both[:, chunk:]
        query_grad = query_scale[c] * (
            query_grad - queries[c] * jnp.sum(queries[c] * query_grad, axis=1, keepdims=True))
        put(first_back, tokens, c, query_grad)
    send_result(0)
    cross = [product(score_grad[c], query[c], TN) for c in chunks]

    if groups > 1:
        @pl.when(group < groups - 1)
        def _():
            copy_back().wait_recv()

        @pl.when(group == groups - 1)
        def _():
            back[...] = jnp.zeros_like(back)

        last_adjoint = jnp.where(back[DK:DK + 1, :] == ids[-1][:, chunk - 1:chunk], back[0:DK, :], 0.0)
    else:
        last_adjoint = jnp.zeros((DK, DK), f32)
    adjoints = [None] * sub
    adjoints[-1] = split(last_adjoint)
    for c in chunks[:-1]:
        adjoints[c] = split(product(to_end[c], adjoints[-1], TN) + own_adjoint[c])

    targets = [product(inv[c], split(direct[c] + product(key_last[c], adjoints[c])), TN) for c in chunks]
    value_grads = [rate[c] * targets[c] for c in chunks]
    for c in chunks:
        put(second_back, 0, c, value_grads[c])
    send_result(1)

    for c in chunks:
        both = product(split(value_grads[c]), both_side[c], NT)
        gram_grad = jnp.where(same[c] & lower, both[:, :chunk], 0.0)
        around = split(-(gram_grad + jnp.transpose(gram_grad)))
        key_grad = (
            product(around, key[c]) - cont[c] * both[:, chunk:] + cross[c]
            + in_last[c] * product(update[c], adjoints[c], NT)
        )
        key_grad = key_scale[c] * (
            key_grad - keys[c] * jnp.sum(keys[c] * key_grad, axis=1, keepdims=True))
        put(second_back, tokens, c, key_grad)
        logit_grad = jnp.sum(targets[c] * updates[c], axis=1, keepdims=True) / (1.0 + jnp.exp(logit[c]))
        logit_rows = jnp.transpose(logit_grad)[0:16, :].astype(bf16)
        for p in range(cores):
            second_back[cores * c + p, 2 * tokens:2 * tokens + 16, :] = logit_rows
    send_result(2)

    for buffer, target in results:
        target[:, columns(me)] = buffer[me]
    for i in range(3):
        for other in others():
            copy_out(i, other, other).wait_recv()
    head_row = lax.broadcasted_iota(jnp.int32, (8, chunk), 0)
    gathered = sum(
        jnp.where(head_row == h, second_out[2 * tokens:2 * tokens + 16, h * DK:(h + 1) * DK].astype(f32)[0:8], 0.0)
        for h in range(count))
    mine = sum(jnp.where(core == p, gathered[:, p * tokens:(p + 1) * tokens], 0.0) for p in range(cores))
    gb_ref[...] = mine.astype(bf16)

    for other in others():
        for i in range(3):
            copy_in(i, other, me).wait_send()
            copy_out(i, other, me).wait_send()
    if groups > 1:
        @pl.when(group < groups - 1)
        def _():
            copy_ahead().wait_send()

        @pl.when(group > 0)
        def _():
            copy_back().wait_send()


def place(first, second, narrow, out, gq, gk, gv, gb, sem):
    tokens = out.shape[0]
    head, tail = pl.ds(0, tokens), pl.ds(tokens, tokens)
    pairs = [
        (first.at[head, :], out), (first.at[tail, :], gq), (second.at[tail, :], gk),
        (second.at[head, :], gv), (narrow, gb)]
    copies = [pltpu.make_async_copy(src, dst, sem.at[i]) for i, (src, dst) in enumerate(pairs)]
    for copy in copies:
        copy.start()
    for copy in copies:
        copy.wait()


def on_device(query, key, value, beta_logit, turn_ids, d_out):
    cores = lax.axis_size("head")
    sub = HEAD_COUNT // cores
    groups = lax.axis_size("ctx") // sub
    tokens = query.shape[0]
    chunk = tokens * cores
    width = query.shape[1]
    wide = jax.ShapeDtypeStruct(query.shape, bf16)
    vmem = pl.BlockSpec(memory_space=pltpu.VMEM)
    anywhere = pl.BlockSpec(memory_space=pl.ANY)
    dma = pltpu.SemaphoreType.DMA
    rows = (tokens + 16, 3 * tokens, 2 * tokens, 2 * tokens + 16)
    state = pltpu.VMEM((DK + 8, DK), f32)
    hbm = pl.BlockSpec(memory_space=pltpu.HBM)
    narrow = jax.ShapeDtypeStruct(beta_logit.shape[::-1], bf16)
    results = pl.pallas_call(
        functools.partial(kernel, groups, sub),
        out_shape=(*(jax.ShapeDtypeStruct((n, width), bf16) for n in rows[2:]), narrow),
        in_specs=[hbm] * 6,
        out_specs=(vmem,) * 3,
        scratch_shapes=[
            pltpu.VMEM((1, chunk), jnp.int32),
            pltpu.VMEM(narrow.shape, bf16),
            *(pltpu.VMEM((n, width), bf16) for n in rows[:2]),
            *(pltpu.VMEM((HEAD_COUNT, n, DK), bf16) for n in rows),
            state, state, state, state,
            *(dma((3, HEAD_COUNT)) for _ in range(4)),
            dma((2,)), dma((2,)), dma((6,)),
        ],
        compiler_params=pltpu.CompilerParams(
            collective_id=0, has_side_effects=True, vmem_limit_bytes=48 * 1024 * 1024),
        cost_estimate=pl.CostEstimate(flops=1_500_000_000, bytes_accessed=2_000_000, transcendentals=100_000),
    )(*(pltpu.with_memory_space_constraint(x, pltpu.HBM) for x in (turn_ids.reshape(1, chunk), beta_logit.T, query, key, value, d_out)))
    results = pl.pallas_call(
        place,
        out_shape=(wide, wide, wide, wide, narrow),
        in_specs=[anywhere] * 3,
        out_specs=(hbm,) * 5,
        scratch_shapes=[dma((5,))],
        cost_estimate=pl.CostEstimate(flops=0, bytes_accessed=1_000_000, transcendentals=0),
    )(*(pltpu.with_memory_space_constraint(x, pltpu.VMEM) for x in results))
    return (*results[:4], results[4].T)


def solution(mesh):
    tokens = P(("grp", "ctx", "head"), None)
    return jax.shard_map(
        on_device,
        mesh=mesh,
        in_specs=(tokens, tokens, tokens, tokens, P(("grp", "ctx")), tokens),
        out_specs=(tokens,) * 5,
        check_vma=False,
    )
```
